32 devices in a mesh: grp: 2 (over x), blk: 16 (over z, y, core).
Axes of the slice: x: 2, y: 2, z: 4, core: 2. Of those that a mesh axis runs over, the one named last changes fastest.
Arguments:
- query_sketch: bfloat16 [16384, 4096], P(('grp', 'blk')), parts along dimension 0, may hold values from -6 to 6
- train_sketch: bfloat16 [4096, 4096], P(('grp', 'blk')), parts along dimension 0, may hold values from -6 to 6
- train_ids: int32 [4096], P(('grp', 'blk')), parts along dimension 0, may hold values from 0 to 2047, each once
- basis_in: bfloat16 [64, 64], P('blk'), may hold values from -0.75 to 0.75
- basis_out: bfloat16 [64, 64], P('blk'), may hold values from -0.75 to 0.75
- eig_in: float32 [64], replicated, may hold values from 0.3 to 3
- eig_out: float32 [64], replicated, may hold values from 0.3 to 3
Outputs:
- scores: float32 [16384, 2048], P(('grp', 'blk')), parts along dimension 0
- totals: float32 [4096], P(('grp', 'blk')), parts along dimension 0
The draws below stay inside these ranges and needn't reach their ends.
There are 2 independent parts, one for each index of `grp`. The reference program is written for one: setup_inputs(seed, part) draws one part's arguments, and reference() takes and returns one part's arrays. A program takes and returns all parts, laid end to end along the dimension named above; an argument that names none is the same for every part. Nothing has to cross between parts.
Inputs may be any that keep to these rules, and one draw needn't show every extreme that they name: `train_ids`: each id appears once in a group.
All inputs are finite; a program needn't handle non-finite values.
Results may differ from the reference program's by a relative error of at most 0.0042.
Values may be sent and summed in bfloat16 or wider, within the bound.
A program may use at most 192 MiB of HBM per device.

```python
import math
import jax
import jax.numpy as jnp
from jax import lax

FOUT = 64
FIN = 64
K = 4096
QUERIES = 8192
NTRAIN = 2048


def block_levels(rng, dims, pieces, low, largest):
    def one(position, shards_of):
        heights = jax.random.uniform(jax.random.fold_in(jax.random.fold_in(rng, 6), position), (shards_of,), jnp.float32, low / len(pieces), largest / len(pieces))
        return jnp.repeat(jnp.exp(heights), dims[position] // shards_of).reshape((-1,) + (1,) * (len(dims) - position - 1))

    level = one(*pieces[0])
    for cut in pieces[1:]:
        level = level * one(*cut)
    return level


def centred(key, dims, deviation, limit, shards=(), kind=jnp.bfloat16):
    factor_of = block_levels(key, dims, shards, -0.22, 0.18) if shards else 1.0
    drawn = jax.random.normal(key, dims, jnp.float32) * deviation * factor_of
    return jnp.minimum(jnp.maximum(drawn, -limit), limit).astype(kind)


def setup_inputs(seed: int = 0, part: int = 0) -> dict:
    splits = jax.random.split(jax.random.key(seed), 8)
    own_keys = jax.random.split(jax.random.fold_in(splits[7], part), 8)
    return {
        "query_sketch": centred(own_keys[0], (QUERIES, K), 1.0, 6.0, ((0, 16),)),
        "train_sketch": centred(own_keys[1], (NTRAIN, K), 1.0, 6.0, ((0, 16),)),
        "train_ids": jax.random.permutation(own_keys[2], NTRAIN).astype(jnp.int32),
        "basis_in": centred(splits[3], (FIN, FIN), FIN ** -0.5, 0.75, ((0, 16),)),
        "basis_out": centred(splits[4], (FOUT, FOUT), FOUT ** -0.5, 0.75, ((0, 16),)),
        "eig_in": jnp.clip(jnp.exp(jax.random.uniform(splits[5], (FIN,), jnp.float32, math.log(0.3), math.log(3.0))), 0.3, 3.0),
        "eig_out": jnp.clip(jnp.exp(jax.random.uniform(splits[6], (FOUT,), jnp.float32, math.log(0.3), math.log(3.0))), 0.3, 3.0),
    }


def rotate(sketch, basis_in, basis_out):
    rows = sketch.shape[0]
    grid = sketch.reshape(rows, FOUT, FIN).astype(jnp.float32)
    half = jnp.einsum('rof,fi->roi', grid, basis_in.astype(jnp.float32)).astype(jnp.bfloat16)
    turned = jnp.einsum('op,roi->rpi', basis_out.astype(jnp.float32), half.astype(jnp.float32))
    return turned.reshape(rows, K)

def reference(query_sketch, train_sketch, train_ids, basis_in, basis_out, eig_in, eig_out):
    eigen_grid = (eig_out[:, None] * eig_in[None, :] + 0.01).reshape(K)
    query_rot = (rotate(query_sketch, basis_in, basis_out) / eigen_grid / jnp.sqrt(jnp.float32(K))).astype(jnp.bfloat16)
    train_rot = rotate(train_sketch, basis_in, basis_out).astype(jnp.bfloat16)
    scores = jnp.dot(query_rot.astype(jnp.float32), train_rot.astype(jnp.float32).T)
    column_sums = lax.optimization_barrier(jnp.sum(scores, axis=0)) / jnp.sqrt(jnp.float32(QUERIES))
    totals = jnp.zeros((NTRAIN,), jnp.float32).at[train_ids].set(column_sums)
    return (scores, totals)
```

```python
import functools

import jax
import jax.numpy as jnp
from jax import lax
from jax.experimental import pallas as pl
from jax.experimental.pallas import tpu as pltpu
from jax.sharding import PartitionSpec as P

FOUT = 64
FIN = 64
LANES = 256
CHUNKS = 4
ITEMS = 4

MESH = pl.DeviceIdType.MESH
BF16 = jnp.bfloat16
F32 = jnp.float32


def dot(a, b, dims=((1,), (0,))):
    return lax.dot_general(a, b, (dims, ((), ())), preferred_element_type=F32)


NT = ((1,), (1,))


def kernel(
    n, lines, q_ref, t_ref, small_ref, scale_ref, scores_ref, totals_ref,
    held, qa, qb, wcol, spread, block_in, stage, factors, smalls, qsum, csum,
    recv, sends, small_recv, small_send, qsum_recv, qsum_send, csum_recv, csum_send,
    local_sem, out_sem,
):
    depth = n // (2 * lines)
    rows = t_ref.shape[0]
    width = t_ref.shape[1]
    piece = rows // CHUNKS
    crossed = CHUNKS // 2 if lines == 2 else 0
    groups = width // LANES
    per = small_ref.shape[0]
    basis_rows = FIN // n
    queries = q_ref.shape[0] * n
    slots = depth * CHUNKS
    spin = 2 * groups // ITEMS

    me = lax.axis_index("blk")
    c = lax.rem(me, 2)
    y = lax.rem(lax.div(me, 2), lines)
    z = lax.div(me, 2 * lines)

    def index(z0, y0, c0):
        return (z0 * lines + y0) * 2 + c0

    q_copy = pltpu.make_async_copy(q_ref, qa, local_sem.at[0])
    q_copy.start()
    own_copy = pltpu.make_async_copy(
        t_ref, held.at[pl.ds(pl.multiple_of(me * rows, rows), rows), :], local_sem.at[1]
    )
    own_copy.start()

    barrier = pltpu.get_barrier_semaphore()

    @pl.loop(1, n)
    def _(j):
        pl.semaphore_signal(
            barrier, inc=1, device_id={"blk": lax.rem(me + j, n)}, device_id_type=MESH
        )

    pl.semaphore_wait(barrier, n - 1)

    def place(s, h):
        return held.at[pl.ds(pl.multiple_of(s * rows + h * piece, piece), piece), :]

    def moved(way, z0, y0, c0, h, target, own=False):
        spot = place(index(z0, y0, c0), h)
        src = t_ref.at[pl.ds(pl.multiple_of(h * piece, piece), piece), :] if own else spot
        return pltpu.make_async_remote_copy(
            src_ref=src,
            dst_ref=spot,
            send_sem=sends.at[way, (z0 * lines + y0) * CHUNKS + h],
            recv_sem=recv.at[index(z0, y0, c0) * CHUNKS + h],
            device_id={"blk": target},
            device_id_type=MESH,
        )

    def ways(z0, y0, h):
        same = y0 == y
        here = jnp.logical_and(y0 != y, jnp.logical_and(z0 == z, h < crossed))
        up = jnp.logical_and(z + 1 < depth, jnp.logical_or(jnp.logical_and(same, z0 <= z), here))
        down = jnp.logical_and(z > 0, jnp.logical_or(jnp.logical_and(same, z0 >= z), here))
        near = jnp.logical_or(z0 == z + 1, z0 == z - 1)
        over = jnp.logical_and(same, jnp.logical_not(jnp.logical_and(near, h < crossed)))
        return up, down, over

    up_target = index(jnp.minimum(z + 1, depth - 1), y, c)
    down_target = index(jnp.maximum(z - 1, 0), y, c)
    over_target = index(z, lines - 1 - y, c)
    twin = index(z, y, 1 - c)

    def send_z(z0, y0, h, own=False):
        up, down, _ = ways(z0, y0, h)

        @pl.when(up)
        def _():
            moved(0, z0, y0, c, h, up_target, own).start()

        @pl.when(down)
        def _():
            moved(1, z0, y0, c, h, down_target, own).start()

    def send_y(z0, y0, h, own=False):
        if lines == 2:

            @pl.when(ways(z0, y0, h)[2])
            def _():
                moved(2, z0, y0, c, h, over_target, own).start()

    def send_twin(z0, y0, h, own=False):
        moved(3, z0, y0, c, h, twin, own).start()

    def arrived(z0, y0, c0, h):
        moved(3, z0, y0, c0, h, twin).wait_recv()

    def order(step):
        both = jnp.minimum(z, depth - 1 - z)
        near = z + (1 - 2 * lax.rem(step, 2)) * (lax.div(step, 2) + 1)
        toward = jnp.where(z < depth - 1 - z, 1, -1)
        return jnp.where(step < 2 * both, near, z + toward * (step - both + 1))

    def to_all(buffer, send_sem, recv_sem, j):
        return pltpu.make_async_remote_copy(
            src_ref=buffer.at[me],
            dst_ref=buffer.at[me],
            send_sem=send_sem.at[j],
            recv_sem=recv_sem.at[me],
            device_id={"blk": lax.rem(me + j, n)},
            device_id_type=MESH,
        )

    def from_one(buffer, send_sem, recv_sem, j):
        s = lax.rem(me + j, n)
        return pltpu.make_async_remote_copy(
            src_ref=buffer.at[s],
            dst_ref=buffer.at[s],
            send_sem=send_sem.at[j],
            recv_sem=recv_sem.at[s],
            device_id={"blk": s},
            device_id_type=MESH,
        )

    def share(buffer, send_sem, recv_sem):
        @pl.loop(1, n)
        def _(j):
            to_all(buffer, send_sem, recv_sem, j).start()

    def collect(buffer, send_sem, recv_sem):
        @pl.loop(1, n)
        def _(j):
            from_one(buffer, send_sem, recv_sem, j).wait_recv()
            to_all(buffer, send_sem, recv_sem, j).wait_send()

    smalls[me] = small_ref[...]
    share(smalls, small_send, small_recv)

    @pl.loop(0, CHUNKS)
    def _(h):
        send_z(z, y, h, own=True)
        send_y(z, y, h, own=True)
        send_twin(z, y, h, own=True)

    collect(smalls, small_send, small_recv)
    for s in range(n):
        factors[s * basis_rows : (s + 1) * basis_rows, :] = smalls[s, 0:basis_rows, :]
    basis_in = factors[:, 0:FIN].astype(BF16)
    basis_out = factors[:, FIN : FIN + FOUT].astype(BF16)

    def hot(test, dims):
        a = lax.broadcasted_iota(jnp.int32, dims, 0)
        b = lax.broadcasted_iota(jnp.int32, dims, 1)
        return test(a, b).astype(F32).astype(BF16)

    repeat = hot(lambda a, b: a % FIN == b, (LANES, FIN))
    alike = hot(lambda a, b: a // FIN == b // FIN, (LANES, LANES)).astype(F32)
    tall = dot(repeat, basis_in).astype(BF16)
    block_in[0] = (dot(tall, repeat, NT) * alike).astype(BF16)
    block_in[1] = (dot(repeat, tall, NT) * alike).astype(BF16)
    unit = hot(lambda a, b: a == b, (FOUT, FOUT))
    turned_out = dot(unit, basis_out, NT).astype(BF16)
    for g in range(groups):
        lanes = slice(g * LANES, (g + 1) * LANES)
        wide = hot(lambda a, b: a == (b + g * LANES) // FIN, (FOUT, LANES))
        spread[0, :, lanes] = dot(basis_out, wide)
        spread[1, :, lanes] = dot(turned_out, wide)

    q_copy.wait()

    def cols(g):
        return pl.ds(pl.multiple_of(g * LANES, LANES), LANES)

    @pl.loop(0, groups)
    def _(g):
        qb[:, cols(g)] = dot(qa[:, cols(g)], block_in[0]).astype(BF16)

    diagonal = (
        lax.broadcasted_iota(jnp.int32, (FIN, LANES), 0)
        == lax.broadcasted_iota(jnp.int32, (FIN, LANES), 1) % FIN
    )

    def fill(which, g):
        for o in range(FOUT):
            row = spread[which, o : o + 1, cols(g)]
            wcol[o * FIN : (o + 1) * FIN, :] = jnp.where(diagonal, row, 0.0).astype(BF16)

    def forward(g):
        fill(0, g)
        qa[:, cols(g)] = (dot(qb[...], wcol[...]) * scale_ref[:, cols(g)]).astype(BF16)

    def back(g):
        fill(1, g)
        middle = dot(qa[...], wcol[...]).astype(BF16)
        final = dot(middle, block_in[1]).astype(BF16)
        qb[:, cols(g)] = final
        qsum[me, :, cols(g)] = jnp.sum(final.astype(F32), axis=0, keepdims=True)

    def out_copy(gi, z0, y0):
        first = pl.multiple_of(index(z0, y0, 0) * rows, 2 * rows)
        slot = lax.rem(gi, 2)
        return pltpu.make_async_copy(
            stage.at[slot], scores_ref.at[:, pl.ds(first, 2 * rows)], out_sem.at[slot]
        )

    def score(gi, z0, y0):
        @pl.loop(0, CHUNKS)
        def _(h):
            arrived(z0, y0, 1 - c, h)

        @pl.when(gi >= 2)
        def _():
            out_copy(gi, z0, y0).wait()

        first = pl.multiple_of(index(z0, y0, 0) * rows, 2 * rows)
        stage[lax.rem(gi, 2)] = dot(qb[...], held[pl.ds(first, 2 * rows), :], NT)
        out_copy(gi, z0, y0).start()

    own_copy.wait()

    @pl.loop(0, slots)
    def _(k):
        step = lax.div(k, CHUNKS)
        h = lax.rem(k, CHUNKS)
        z_line = order(step)

        @pl.when(step < depth - 1)
        def _():
            arrived(z_line, y, c, h)
            send_z(z_line, y, h)
            send_y(z_line, y, h)
            send_twin(z_line, y, h)

        if lines == 2:
            z_cross = jnp.where(step == 0, z, order(step - 1))
            by_z = jnp.logical_and(
                jnp.logical_or(z_cross == z + 1, z_cross == z - 1), h < crossed
            )

            @pl.when(jnp.logical_not(by_z))
            def _():
                arrived(z_cross, 1 - y, c, h)
                send_twin(z_cross, 1 - y, h)

            @pl.when(k == slots - CHUNKS)
            def _():
                @pl.loop(0, crossed)
                def _(i):
                    send_z(z, 1 - y, i)

        @pl.when(k < spin // 2)
        def _():
            @pl.loop(0, ITEMS)
            def _(i):
                forward(k * ITEMS + i)

        @pl.when(jnp.logical_and(k >= spin // 2, k < spin))
        def _():
            @pl.loop(0, ITEMS)
            def _(i):
                back((k - spin // 2) * ITEMS + i)

        @pl.when(k == spin)
        def _():
            share(qsum, qsum_send, qsum_recv)

        @pl.when(k == spin + 2)
        def _():
            collect(qsum, qsum_send, qsum_recv)
            total = qsum[0]
            for s in range(1, n):
                total = total + qsum[s]
            high = total.astype(BF16)
            rest = total - high.astype(F32)
            middle = rest.astype(BF16)
            low = (rest - middle.astype(F32)).astype(BF16)
            mine = held[pl.ds(pl.multiple_of(me * rows, rows), rows), :]
            count = 16
            sums = jnp.zeros((1, rows), F32)
            for part in (low, middle, high):
                full = jnp.broadcast_to(part.astype(F32), (count, width)).astype(BF16)
                sums = sums + dot(full, mine, NT)[0:1, :]
            csum[me] = sums * (1.0 / float(queries) ** 0.5)
            share(csum, csum_send, csum_recv)

        early = k - spin
        use_own = early == 0
        use_first = jnp.logical_and(early >= 1, early <= 2)
        use_line = jnp.logical_and(
            early >= 3, jnp.logical_and(h == CHUNKS - 1, step < depth - 1)
        )
        chosen = jnp.where(use_first, early - 1, step)
        z_score = jnp.where(use_own, z, order(chosen))
        gi = jnp.where(use_own, 0, chosen + 1)
        use = jnp.logical_or(use_own, jnp.logical_or(use_first, use_line))
        y_score = y
        if lines == 2:
            use_cross = k == slots - CHUNKS
            z_score = jnp.where(use_cross, z, z_score)
            y_score = jnp.where(use_cross, 1 - y, y)
            gi = jnp.where(use_cross, depth, gi)
            use = jnp.logical_or(use, use_cross)

        @pl.when(use)
        def _():
            score(gi, z_score, y_score)

    if lines == 2:
        for side in (1, -1):

            @pl.when(jnp.logical_and(z + side >= 0, z + side < depth))
            def _():
                @pl.loop(0, crossed)
                def _(h):
                    arrived(z + side, 1 - y, c, h)
                    send_twin(z + side, 1 - y, h)

        @pl.loop(0, depth - 1)
        def _(j):
            score(depth + 1 + j, order(depth - 2 - j), 1 - y)

    collect(csum, csum_send, csum_recv)
    ids = (
        lax.broadcasted_iota(jnp.int32, (rows, rows), 0) + me * rows
    ).astype(F32)
    picked = jnp.zeros((rows, rows), F32)
    for s in range(n):
        picked = picked + jnp.where(smalls[s, per - 1 : per, :] == ids, csum[s], 0.0)
    totals_ref[...] = jnp.sum(picked.T, axis=0, keepdims=True)

    done = depth * lines
    out_copy(done, z, y).wait()
    out_copy(done + 1, z, y).wait()

    @pl.loop(0, depth * lines)
    def _(s):
        z0 = lax.div(s, lines)
        y0 = lax.rem(s, lines)

        @pl.loop(0, CHUNKS)
        def _(h):
            up, down, over = ways(z0, y0, h)

            @pl.when(up)
            def _():
                moved(0, z0, y0, c, h, up_target).wait_send()

            @pl.when(down)
            def _():
                moved(1, z0, y0, c, h, down_target).wait_send()

            if lines == 2:

                @pl.when(over)
                def _():
                    moved(2, z0, y0, c, h, over_target).wait_send()

            moved(3, z0, y0, c, h, twin).wait_send()


def per_device(n, lines, query_sketch, train_sketch, train_ids, basis_in, basis_out, eig_in, eig_out):
    width = FOUT * FIN
    queries, rows = query_sketch.shape[0], train_sketch.shape[0]
    scale = (
        1.0 / (eig_out[:, None] * eig_in[None, :] + 0.01) / jnp.sqrt(jnp.float32(width))
    ).reshape(1, width)
    both = jnp.concatenate([basis_in, basis_out], axis=1).astype(F32)
    small = jnp.concatenate(
        [both, jnp.zeros((7 - both.shape[0], 128), F32), train_ids.astype(F32)[None, :]], axis=0
    )
    sources = n // 2
    dma = pltpu.SemaphoreType.DMA
    vmem = pl.BlockSpec(memory_space=pltpu.VMEM)
    hbm = pl.BlockSpec(memory_space=pl.ANY)
    scores, totals = pl.pallas_call(
        functools.partial(kernel, n, lines),
        out_shape=(
            jax.ShapeDtypeStruct((queries, rows * n), F32),
            jax.ShapeDtypeStruct((1, rows), F32),
        ),
        in_specs=[hbm, hbm, vmem, vmem],
        out_specs=(hbm, vmem),
        scratch_shapes=[
            pltpu.VMEM((n * rows, width), BF16),
            pltpu.VMEM((queries, width), BF16),
            pltpu.VMEM((queries, width), BF16),
            pltpu.VMEM((width, LANES), BF16),
            pltpu.VMEM((2, FOUT, width), F32),
            pltpu.VMEM((2, LANES, LANES), BF16),
            pltpu.VMEM((2, queries, 2 * rows), F32),
            pltpu.VMEM((FIN, 128), F32),
            pltpu.VMEM((n, 8, 128), F32),
            pltpu.VMEM((n, 1, width), F32),
            pltpu.VMEM((n, 1, rows), F32),
            dma((n * CHUNKS,)),
            dma((4, sources * CHUNKS)),
            dma((n,)),
            dma((n,)),
            dma((n,)),
            dma((n,)),
            dma((n,)),
            dma((n,)),
            dma((2,)),
            dma((2,)),
        ],
        compiler_params=pltpu.CompilerParams(
            collective_id=0, has_side_effects=True, vmem_limit_bytes=58 * 1024 * 1024
        ),
        cost_estimate=pl.CostEstimate(
            flops=2 * queries * width * (rows * n + 2 * width),
            bytes_accessed=2 * queries * width + 4 * queries * rows * n,
            transcendentals=0,
        ),
    )(query_sketch, train_sketch, small, scale)
    return scores, totals.reshape(rows)


def solution(mesh):
    placed = (
        P(("grp", "blk"), None),
        P(("grp", "blk"), None),
        P(("grp", "blk")),
        P("blk", None),
        P("blk", None),
        P(),
        P(),
    )
    lines = 2 if mesh.shape["grp"] == 2 else 1
    return jax.shard_map(
        functools.partial(per_device, mesh.shape["blk"], lines),
        mesh=mesh,
        in_specs=placed,
        out_specs=(P(("grp", "blk"), None), P(("grp", "blk"))),
        check_vma=False,
    )
```

```python
import functools

import jax
import jax.numpy as jnp
from jax import lax
from jax.experimental import pallas as pl
from jax.experimental.pallas import tpu as pltpu
from jax.sharding import PartitionSpec as P

FOUT = 64
FIN = 64
LANES = 256
CHUNKS = 4
ITEMS = 4

MESH = pl.DeviceIdType.MESH
BF16 = jnp.bfloat16
F32 = jnp.float32


def dot(a, b, dims=((1,), (0,))):
    return lax.dot_general(a, b, (dims, ((), ())), preferred_element_type=F32)


NT = ((1,), (1,))


def kernel(
    n, lines, q_ref, t_ref, in_ref, out_ref, ids_ref, eig_in_ref, eig_out_ref, scores_ref, totals_ref,
    held, qa, qb, wcol, spread, scale, block_in, stage, factors, smalls, qsum, qpart, qtotal, csum,
    recv, sends, small_recv, small_send, qpart_recv, qpart_send, qsum_recv, qsum_send, csum_recv,
    csum_send,
    local_sem, out_sem,
):
    depth = n // (2 * lines)
    rows = t_ref.shape[0]
    width = t_ref.shape[1]
    piece = rows // CHUNKS
    crossed = CHUNKS // 2 if lines == 2 else 0
    groups = width // LANES
    per = smalls.shape[1]
    slab = width // n
    basis_rows = FIN // n
    queries = q_ref.shape[0] * n
    slots = depth * CHUNKS
    spin = 2 * groups // ITEMS

    me = lax.axis_index("blk")
    c = lax.rem(me, 2)
    y = lax.rem(lax.div(me, 2), lines)
    z = lax.div(me, 2 * lines)

    def index(z0, y0, c0):
        return (z0 * lines + y0) * 2 + c0

    q_copy = pltpu.make_async_copy(q_ref, qa, local_sem.at[0])
    q_copy.start()
    own_copy = pltpu.make_async_copy(
        t_ref, held.at[pl.ds(pl.multiple_of(me * rows, rows), rows), :], local_sem.at[1]
    )
    own_copy.start()

    barrier = pltpu.get_barrier_semaphore()

    @pl.loop(1, n)
    def _(j):
        pl.semaphore_signal(
            barrier, inc=1, device_id={"blk": lax.rem(me + j, n)}, device_id_type=MESH
        )

    pl.semaphore_wait(barrier, n - 1)

    def place(s, h):
        return held.at[pl.ds(pl.multiple_of(s * rows + h * piece, piece), piece), :]

    def moved(way, z0, y0, c0, h, target, own=False):
        spot = place(index(z0, y0, c0), h)
        src = t_ref.at[pl.ds(pl.multiple_of(h * piece, piece), piece), :] if own else spot
        return pltpu.make_async_remote_copy(
            src_ref=src,
            dst_ref=spot,
            send_sem=sends.at[way, (z0 * lines + y0) * CHUNKS + h],
            recv_sem=recv.at[index(z0, y0, c0) * CHUNKS + h],
            device_id={"blk": target},
            device_id_type=MESH,
        )

    def ways(z0, y0, h):
        same = y0 == y
        here = jnp.logical_and(y0 != y, jnp.logical_and(z0 == z, h < crossed))
        up = jnp.logical_and(z + 1 < depth, jnp.logical_or(jnp.logical_and(same, z0 <= z), here))
        down = jnp.logical_and(z > 0, jnp.logical_or(jnp.logical_and(same, z0 >= z), here))
        near = jnp.logical_or(z0 == z + 1, z0 == z - 1)
        over = jnp.logical_and(same, jnp.logical_not(jnp.logical_and(near, h < crossed)))
        return up, down, over

    up_target = index(jnp.minimum(z + 1, depth - 1), y, c)
    down_target = index(jnp.maximum(z - 1, 0), y, c)
    over_target = index(z, lines - 1 - y, c)
    twin = index(z, y, 1 - c)

    def send_z(z0, y0, h, own=False):
        up, down, _ = ways(z0, y0, h)

        @pl.when(up)
        def _():
            moved(0, z0, y0, c, h, up_target, own).start()

        @pl.when(down)
        def _():
            moved(1, z0, y0, c, h, down_target, own).start()

    def send_y(z0, y0, h, own=False):
        if lines == 2:

            @pl.when(ways(z0, y0, h)[2])
            def _():
                moved(2, z0, y0, c, h, over_target, own).start()

    def send_twin(z0, y0, h, own=False):
        moved(3, z0, y0, c, h, twin, own).start()

    def arrived(z0, y0, c0, h):
        moved(3, z0, y0, c0, h, twin).wait_recv()

    def inside(z0):
        return jnp.logical_and(z0 >= 0, z0 < depth)

    def to_all(buffer, send_sem, recv_sem, j):
        return pltpu.make_async_remote_copy(
            src_ref=buffer.at[me],
            dst_ref=buffer.at[me],
            send_sem=send_sem.at[j],
            recv_sem=recv_sem.at[me],
            device_id={"blk": lax.rem(me + j, n)},
            device_id_type=MESH,
        )

    def from_one(buffer, send_sem, recv_sem, j):
        s = lax.rem(me + j, n)
        return pltpu.make_async_remote_copy(
            src_ref=buffer.at[s],
            dst_ref=buffer.at[s],
            send_sem=send_sem.at[j],
            recv_sem=recv_sem.at[s],
            device_id={"blk": s},
            device_id_type=MESH,
        )

    def share(buffer, send_sem, recv_sem):
        @pl.loop(1, n)
        def _(j):
            to_all(buffer, send_sem, recv_sem, j).start()

    def collect(buffer, send_sem, recv_sem):
        @pl.loop(1, n)
        def _(j):
            from_one(buffer, send_sem, recv_sem, j).wait_recv()
            to_all(buffer, send_sem, recv_sem, j).wait_send()

    smalls[me] = jnp.zeros(smalls.shape[1:], F32)
    smalls[me, 0:basis_rows, 0:FIN] = in_ref[...].astype(F32)
    smalls[me, 0:basis_rows, FIN : FIN + FOUT] = out_ref[...].astype(F32)
    smalls[me, per - 1 : per, :] = ids_ref[...].astype(F32)
    share(smalls, small_send, small_recv)

    @pl.loop(0, CHUNKS)
    def _(h):
        send_z(z, y, h, own=True)
        send_y(z, y, h, own=True)
        send_twin(z, y, h, own=True)

    for o in range(FOUT):
        grid = eig_out_ref[0, o] * eig_in_ref[...] + 0.01
        scale[:, o * FIN : (o + 1) * FIN] = 1.0 / grid / (float(width) ** 0.5)
    collect(smalls, small_send, small_recv)
    for s in range(n):
        factors[s * basis_rows : (s + 1) * basis_rows, :] = smalls[s, 0:basis_rows, :]
    basis_in = factors[:, 0:FIN].astype(BF16)
    basis_out = factors[:, FIN : FIN + FOUT].astype(BF16)

    def hot(test, dims):
        a = lax.broadcasted_iota(jnp.int32, dims, 0)
        b = lax.broadcasted_iota(jnp.int32, dims, 1)
        return test(a, b).astype(F32).astype(BF16)

    repeat = hot(lambda a, b: a % FIN == b, (LANES, FIN))
    alike = hot(lambda a, b: a // FIN == b // FIN, (LANES, LANES)).astype(F32)
    tall = dot(repeat, basis_in).astype(BF16)
    block_in[0] = (dot(tall, repeat, NT) * alike).astype(BF16)
    block_in[1] = (dot(repeat, tall, NT) * alike).astype(BF16)
    unit = hot(lambda a, b: a == b, (FOUT, FOUT))
    turned_out = dot(unit, basis_out, NT).astype(BF16)
    for g in range(groups):
        lanes = slice(g * LANES, (g + 1) * LANES)
        wide = hot(lambda a, b: a == (b + g * LANES) // FIN, (FOUT, LANES))
        spread[0, :, lanes] = dot(basis_out, wide)
        spread[1, :, lanes] = dot(turned_out, wide)

    q_copy.wait()

    def cols(g):
        return pl.ds(pl.multiple_of(g * LANES, LANES), LANES)

    @pl.loop(0, groups)
    def _(g):
        qb[:, cols(g)] = dot(qa[:, cols(g)], block_in[0]).astype(BF16)

    diagonal = (
        lax.broadcasted_iota(jnp.int32, (FIN, LANES), 0)
        == lax.broadcasted_iota(jnp.int32, (FIN, LANES), 1) % FIN
    )

    def fill(which, g):
        for o in range(FOUT):
            row = spread[which, o : o + 1, cols(g)]
            wcol[o * FIN : (o + 1) * FIN, :] = jnp.where(diagonal, row, 0.0).astype(BF16)

    def forward(g):
        fill(0, g)
        qa[:, cols(g)] = (dot(qb[...], wcol[...]) * scale[:, cols(g)]).astype(BF16)

    def back(g):
        fill(1, g)
        middle = dot(qa[...], wcol[...]).astype(BF16)
        final = dot(middle, block_in[1]).astype(BF16)
        qb[:, cols(g)] = final
        column = jnp.sum(final.astype(F32), axis=0, keepdims=True)
        for i in range(LANES // slab):
            qsum[g * (LANES // slab) + i] = column[:, i * slab : (i + 1) * slab]

    def part_to(j):
        s = lax.rem(me + j, n)
        return pltpu.make_async_remote_copy(
            src_ref=qsum.at[s],
            dst_ref=qpart.at[me],
            send_sem=qpart_send.at[j],
            recv_sem=qpart_recv.at[me],
            device_id={"blk": s},
            device_id_type=MESH,
        )

    def out_copy(z0, y0):
        first = pl.multiple_of(index(z0, y0, 0) * rows, 2 * rows)
        slot = z0 * lines + y0
        return pltpu.make_async_copy(
            stage.at[slot], scores_ref.at[:, pl.ds(first, 2 * rows)], out_sem.at[slot]
        )

    def score(far, y0):
        @pl.loop(0, 2)
        def _(i):
            z0 = z + (1 - 2 * i) * far

            @pl.when(jnp.logical_and(inside(z0), jnp.logical_or(i == 0, far > 0)))
            def _():
                @pl.loop(0, CHUNKS)
                def _(h):
                    arrived(z0, y0, 1 - c, h)

                first = pl.multiple_of(index(z0, y0, 0) * rows, 2 * rows)
                stage[z0 * lines + y0] = dot(qb[...], held[pl.ds(first, 2 * rows), :], NT)
                out_copy(z0, y0).start()

    own_copy.wait()

    @pl.loop(0, slots)
    def _(k):
        step = lax.div(k, CHUNKS)
        h = lax.rem(k, CHUNKS)
        for side in (1, -1):
            z_line = z + side * (step + 1)

            @pl.when(inside(z_line))
            def _():
                arrived(z_line, y, c, h)
                send_z(z_line, y, h)
                send_y(z_line, y, h)
                send_twin(z_line, y, h)

        if lines == 2:
            for side in (1, -1):
                z_cross = z + side * step
                wanted = jnp.logical_or(step > 1, jnp.logical_or(step == 0, h >= crossed))
                if side == -1:
                    wanted = jnp.logical_and(wanted, step > 0)

                @pl.when(jnp.logical_and(wanted, inside(z_cross)))
                def _():
                    arrived(z_cross, 1 - y, c, h)
                    send_twin(z_cross, 1 - y, h)

            @pl.when(k == slots - CHUNKS)
            def _():
                @pl.loop(0, crossed)
                def _(i):
                    send_z(z, 1 - y, i)

        @pl.when(k < spin // 2)
        def _():
            @pl.loop(0, ITEMS)
            def _(i):
                forward(k * ITEMS + i)

        @pl.when(jnp.logical_and(k >= spin // 2, k < spin))
        def _():
            @pl.loop(0, ITEMS)
            def _(i):
                back((k - spin // 2) * ITEMS + i)

        @pl.when(k == spin)
        def _():
            @pl.loop(1, n)
            def _(j):
                part_to(j).start()

        @pl.when(k == spin + 1)
        def _():
            @pl.loop(1, n)
            def _(j):
                s = lax.rem(me + j, n)
                pltpu.make_async_remote_copy(
                    src_ref=qsum.at[s],
                    dst_ref=qpart.at[s],
                    send_sem=qpart_send.at[j],
                    recv_sem=qpart_recv.at[s],
                    device_id={"blk": s},
                    device_id_type=MESH,
                ).wait_recv()
                part_to(j).wait_send()

            qpart[me] = qsum[me]
            added = qpart[0]
            for s in range(1, n):
                added = added + qpart[s]
            qtotal[me] = added
            share(qtotal, qsum_send, qsum_recv)

        @pl.when(k == spin + 2)
        def _():
            collect(qtotal, qsum_send, qsum_recv)
            total = jnp.concatenate([qtotal[s] for s in range(n)], axis=1)
            high = total.astype(BF16)
            rest = total - high.astype(F32)
            middle = rest.astype(BF16)
            low = (rest - middle.astype(F32)).astype(BF16)
            mine = held[pl.ds(pl.multiple_of(me * rows, rows), rows), :]
            count = 16
            sums = jnp.zeros((1, rows), F32)
            for part in (low, middle, high):
                full = jnp.broadcast_to(part.astype(F32), (count, width)).astype(BF16)
                sums = sums + dot(full, mine, NT)[0:1, :]
            csum[me] = sums * (1.0 / float(queries) ** 0.5)
            share(csum, csum_send, csum_recv)

        early = k - spin
        by_arrival = jnp.logical_and(
            early > 2, jnp.logical_and(h == CHUNKS - 1, step + 1 < depth)
        )
        far = jnp.where(early > 2, step + 1, early)
        use = jnp.logical_or(jnp.logical_and(early >= 0, early <= 2), by_arrival)
        y_score = y
        if lines == 2:
            other = jnp.logical_or(k == spin + CHUNKS, k == spin + CHUNKS + 1)
            far = jnp.where(k == spin + CHUNKS, 0, jnp.where(k == spin + CHUNKS + 1, 2, far))
            y_score = jnp.where(other, 1 - y, y)
            use = jnp.logical_or(use, other)

        @pl.when(use)
        def _():
            score(far, y_score)

    if lines == 2:
        for side in (1, -1):

            @pl.when(jnp.logical_and(z + side >= 0, z + side < depth))
            def _():
                @pl.loop(0, crossed)
                def _(h):
                    arrived(z + side, 1 - y, c, h)
                    send_twin(z + side, 1 - y, h)

        @pl.loop(0, 2)
        def _(j):
            score(3 - 2 * j, 1 - y)

    collect(csum, csum_send, csum_recv)
    ids = (
        lax.broadcasted_iota(jnp.int32, (rows, rows), 0) + me * rows
    ).astype(F32)
    picked = jnp.zeros((rows, rows), F32)
    for s in range(n):
        picked = picked + jnp.where(smalls[s, per - 1 : per, :] == ids, csum[s], 0.0)
    totals_ref[...] = jnp.sum(picked.T, axis=0, keepdims=True)

    @pl.loop(0, depth * lines)
    def _(s):
        z0 = lax.div(s, lines)
        y0 = lax.rem(s, lines)
        out_copy(z0, y0).wait()

        @pl.loop(0, CHUNKS)
        def _(h):
            up, down, over = ways(z0, y0, h)

            @pl.when(up)
            def _():
                moved(0, z0, y0, c, h, up_target).wait_send()

            @pl.when(down)
            def _():
                moved(1, z0, y0, c, h, down_target).wait_send()

            if lines == 2:

                @pl.when(over)
                def _():
                    moved(2, z0, y0, c, h, over_target).wait_send()

            moved(3, z0, y0, c, h, twin).wait_send()


def per_device(n, lines, query_sketch, train_sketch, train_ids, basis_in, basis_out, eig_in, eig_out):
    width = FOUT * FIN
    queries, rows = query_sketch.shape[0], train_sketch.shape[0]
    sources = n // 2
    dma = pltpu.SemaphoreType.DMA
    vmem = pl.BlockSpec(memory_space=pltpu.VMEM)
    hbm = pl.BlockSpec(memory_space=pl.ANY)
    scores, totals = pl.pallas_call(
        functools.partial(kernel, n, lines),
        out_shape=(
            jax.ShapeDtypeStruct((queries, rows * n), F32),
            jax.ShapeDtypeStruct((1, rows), F32),
        ),
        in_specs=[hbm, hbm, vmem, vmem, vmem, vmem, pl.BlockSpec(memory_space=pltpu.SMEM)],
        out_specs=(hbm, vmem),
        scratch_shapes=[
            pltpu.VMEM((n * rows, width), BF16),
            pltpu.VMEM((queries, width), BF16),
            pltpu.VMEM((queries, width), BF16),
            pltpu.VMEM((width, LANES), BF16),
            pltpu.VMEM((2, FOUT, width), F32),
            pltpu.VMEM((1, width), F32),
            pltpu.VMEM((2, LANES, LANES), BF16),
            pltpu.VMEM((sources, queries, 2 * rows), F32),
            pltpu.VMEM((FIN, 128), F32),
            pltpu.VMEM((n, 8, 128), F32),
            pltpu.VMEM((n, 1, width // n), F32),
            pltpu.VMEM((n, 1, width // n), F32),
            pltpu.VMEM((n, 1, width // n), F32),
            pltpu.VMEM((n, 1, rows), F32),
            dma((n * CHUNKS,)),
            dma((4, sources * CHUNKS)),
            dma((n,)),
            dma((n,)),
            dma((n,)),
            dma((n,)),
            dma((n,)),
            dma((n,)),
            dma((n,)),
            dma((n,)),
            dma((2,)),
            dma((sources,)),
        ],
        compiler_params=pltpu.CompilerParams(
            collective_id=0, has_side_effects=True, vmem_limit_bytes=58 * 1024 * 1024
        ),
        cost_estimate=pl.CostEstimate(
            flops=2 * queries * width * (rows * n + 2 * width),
            bytes_accessed=2 * queries * width + 4 * queries * rows * n,
            transcendentals=0,
        ),
    )(
        query_sketch, train_sketch, basis_in, basis_out,
        train_ids.reshape(1, rows), eig_in.reshape(1, FIN), eig_out.reshape(1, FOUT),
    )
    return scores, totals.reshape(rows)


def solution(mesh):
    placed = (
        P(("grp", "blk"), None),
        P(("grp", "blk"), None),
        P(("grp", "blk")),
        P("blk", None),
        P("blk", None),
        P(),
        P(),
    )
    lines = 2 if mesh.shape["grp"] == 2 else 1
    return jax.shard_map(
        functools.partial(per_device, mesh.shape["blk"], lines),
        mesh=mesh,
        in_specs=placed,
        out_specs=(P(("grp", "blk"), None), P(("grp", "blk"))),
        check_vma=False,
    )
```

```python
import functools

import jax
import jax.numpy as jnp
from jax import lax
from jax.experimental import pallas as pl
from jax.experimental.pallas import tpu as pltpu
from jax.sharding import PartitionSpec as P

FOUT = 64
FIN = 64
LANES = 256
CHUNKS = 4
ITEMS = 4

MESH = pl.DeviceIdType.MESH
BF16 = jnp.bfloat16
F32 = jnp.float32


def dot(a, b, dims=((1,), (0,))):
    return lax.dot_general(a, b, (dims, ((), ())), preferred_element_type=F32)


NT = ((1,), (1,))


def kernel(
    n, lines, q_ref, t_ref, in_ref, out_ref, ids_ref, eig_in_ref, eig_out_ref, scores_ref, totals_ref,
    held, qa, qb, wcol, spread, scale, block_in, stage, factors, smalls, qsum, qpart, qtotal, csum,
    recv, sends, small_recv, small_send, qpart_recv, qpart_send, qsum_recv, qsum_send, csum_recv,
    csum_send,
    local_sem, out_sem,
):
    depth = n // (2 * lines)
    rows = t_ref.shape[0]
    width = t_ref.shape[1]
    piece = rows // CHUNKS
    crossed = CHUNKS // 2 if lines == 2 else 0
    groups = width // LANES
    per = smalls.shape[1]
    slab = width // n
    basis_rows = FIN // n
    queries = q_ref.shape[0] * n
    slots = depth * CHUNKS
    spin = 2 * groups // ITEMS

    me = lax.axis_index("blk")
    c = lax.rem(me, 2)
    y = lax.rem(lax.div(me, 2), lines)
    z = lax.div(me, 2 * lines)

    def index(z0, y0, c0):
        return (z0 * lines + y0) * 2 + c0

    q_copy = pltpu.make_async_copy(q_ref, qa, local_sem.at[0])
    q_copy.start()
    own_copy = pltpu.make_async_copy(
        t_ref, held.at[pl.ds(pl.multiple_of(me * rows, rows), rows), :], local_sem.at[1]
    )
    own_copy.start()

    barrier = pltpu.get_barrier_semaphore()

    @pl.loop(1, n)
    def _(j):
        pl.semaphore_signal(
            barrier, inc=1, device_id={"blk": lax.rem(me + j, n)}, device_id_type=MESH
        )

    pl.semaphore_wait(barrier, n - 1)

    def place(s, h):
        return held.at[pl.ds(pl.multiple_of(s * rows + h * piece, piece), piece), :]

    def moved(way, z0, y0, c0, h, target, own=False):
        spot = place(index(z0, y0, c0), h)
        src = t_ref.at[pl.ds(pl.multiple_of(h * piece, piece), piece), :] if own else spot
        return pltpu.make_async_remote_copy(
            src_ref=src,
            dst_ref=spot,
            send_sem=sends.at[way, (z0 * lines + y0) * CHUNKS + h],
            recv_sem=recv.at[index(z0, y0, c0) * CHUNKS + h],
            device_id={"blk": target},
            device_id_type=MESH,
        )

    def ways(z0, y0, h):
        same = y0 == y
        here = jnp.logical_and(y0 != y, jnp.logical_and(z0 == z, h < crossed))
        up = jnp.logical_and(z + 1 < depth, jnp.logical_or(jnp.logical_and(same, z0 <= z), here))
        down = jnp.logical_and(z > 0, jnp.logical_or(jnp.logical_and(same, z0 >= z), here))
        near = jnp.logical_or(z0 == z + 1, z0 == z - 1)
        over = jnp.logical_and(same, jnp.logical_not(jnp.logical_and(near, h < crossed)))
        return up, down, over

    up_target = index(jnp.minimum(z + 1, depth - 1), y, c)
    down_target = index(jnp.maximum(z - 1, 0), y, c)
    over_target = index(z, lines - 1 - y, c)
    twin = index(z, y, 1 - c)

    def send_z(z0, y0, h, own=False):
        up, down, _ = ways(z0, y0, h)

        @pl.when(up)
        def _():
            moved(0, z0, y0, c, h, up_target, own).start()

        @pl.when(down)
        def _():
            moved(1, z0, y0, c, h, down_target, own).start()

    def send_y(z0, y0, h, own=False):
        if lines == 2:

            @pl.when(ways(z0, y0, h)[2])
            def _():
                moved(2, z0, y0, c, h, over_target, own).start()

    def send_twin(z0, y0, h, own=False):
        moved(3, z0, y0, c, h, twin, own).start()

    def arrived(z0, y0, c0, h):
        moved(3, z0, y0, c0, h, twin).wait_recv()

    def inside(z0):
        return jnp.logical_and(z0 >= 0, z0 < depth)

    def to_all(buffer, send_sem, recv_sem, j):
        return pltpu.make_async_remote_copy(
            src_ref=buffer.at[me],
            dst_ref=buffer.at[me],
            send_sem=send_sem.at[j],
            recv_sem=recv_sem.at[me],
            device_id={"blk": lax.rem(me + j, n)},
            device_id_type=MESH,
        )

    def from_one(buffer, send_sem, recv_sem, j):
        s = lax.rem(me + j, n)
        return pltpu.make_async_remote_copy(
            src_ref=buffer.at[s],
            dst_ref=buffer.at[s],
            send_sem=send_sem.at[j],
            recv_sem=recv_sem.at[s],
            device_id={"blk": s},
            device_id_type=MESH,
        )

    def share(buffer, send_sem, recv_sem):
        @pl.loop(1, n)
        def _(j):
            to_all(buffer, send_sem, recv_sem, j).start()

    def collect(buffer, send_sem, recv_sem):
        @pl.loop(1, n)
        def _(j):
            from_one(buffer, send_sem, recv_sem, j).wait_recv()
            to_all(buffer, send_sem, recv_sem, j).wait_send()

    smalls[me] = jnp.zeros(smalls.shape[1:], F32)
    smalls[me, 0:basis_rows, 0:FIN] = in_ref[...].astype(F32)
    smalls[me, 0:basis_rows, FIN : FIN + FOUT] = out_ref[...].astype(F32)
    smalls[me, per - 1 : per, :] = ids_ref[...].astype(F32)
    share(smalls, small_send, small_recv)

    @pl.loop(0, CHUNKS)
    def _(h):
        send_z(z, y, h, own=True)
        send_y(z, y, h, own=True)
        send_twin(z, y, h, own=True)

    for o in range(FOUT):
        grid = eig_out_ref[0, o] * eig_in_ref[...] + 0.01
        scale[:, o * FIN : (o + 1) * FIN] = 1.0 / grid / (float(width) ** 0.5)
    collect(smalls, small_send, small_recv)
    for s in range(n):
        factors[s * basis_rows : (s + 1) * basis_rows, :] = smalls[s, 0:basis_rows, :]
    basis_in = factors[:, 0:FIN].astype(BF16)
    basis_out = factors[:, FIN : FIN + FOUT].astype(BF16)

    def hot(test, dims):
        a = lax.broadcasted_iota(jnp.int32, dims, 0)
        b = lax.broadcasted_iota(jnp.int32, dims, 1)
        return test(a, b).astype(F32).astype(BF16)

    repeat = hot(lambda a, b: a % FIN == b, (LANES, FIN))
    alike = hot(lambda a, b: a // FIN == b // FIN, (LANES, LANES)).astype(F32)
    tall = dot(repeat, basis_in).astype(BF16)
    block_in[0] = (dot(tall, repeat, NT) * alike).astype(BF16)
    block_in[1] = (dot(repeat, tall, NT) * alike).astype(BF16)
    unit = hot(lambda a, b: a == b, (FOUT, FOUT))
    turned_out = dot(unit, basis_out, NT).astype(BF16)
    for g in range(groups):
        lanes = slice(g * LANES, (g + 1) * LANES)
        wide = hot(lambda a, b: a == (b + g * LANES) // FIN, (FOUT, LANES))
        spread[0, :, lanes] = dot(basis_out, wide)
        spread[1, :, lanes] = dot(turned_out, wide)

    q_copy.wait()

    def cols(g):
        return pl.ds(pl.multiple_of(g * LANES, LANES), LANES)

    @pl.loop(0, groups)
    def _(g):
        qb[:, cols(g)] = dot(qa[:, cols(g)], block_in[0]).astype(BF16)

    diagonal = (
        lax.broadcasted_iota(jnp.int32, (FIN, LANES), 0)
        == lax.broadcasted_iota(jnp.int32, (FIN, LANES), 1) % FIN
    )

    def fill(which, g):
        for o in range(FOUT):
            row = spread[which, o : o + 1, cols(g)]
            wcol[o * FIN : (o + 1) * FIN, :] = jnp.where(diagonal, row, 0.0).astype(BF16)

    def forward(g):
        fill(0, g)
        qa[:, cols(g)] = (dot(qb[...], wcol[...]) * scale[:, cols(g)]).astype(BF16)

    def back(g):
        fill(1, g)
        middle = dot(qa[...], wcol[...]).astype(BF16)
        final = dot(middle, block_in[1]).astype(BF16)
        qb[:, cols(g)] = final
        column = jnp.sum(final.astype(F32), axis=0, keepdims=True)
        for i in range(LANES // slab):
            qsum[g * (LANES // slab) + i] = column[:, i * slab : (i + 1) * slab]

    def part_to(j):
        s = lax.rem(me + j, n)
        return pltpu.make_async_remote_copy(
            src_ref=qsum.at[s],
            dst_ref=qpart.at[me],
            send_sem=qpart_send.at[j],
            recv_sem=qpart_recv.at[me],
            device_id={"blk": s},
            device_id_type=MESH,
        )

    def out_copy(z0, y0):
        first = pl.multiple_of(index(z0, y0, 0) * rows, 2 * rows)
        slot = z0 * lines + y0
        return pltpu.make_async_copy(
            stage.at[slot], scores_ref.at[:, pl.ds(first, 2 * rows)], out_sem.at[slot]
        )

    def score(far, y0):
        @pl.loop(0, 2)
        def _(i):
            z0 = z + (1 - 2 * i) * far

            @pl.when(jnp.logical_and(inside(z0), jnp.logical_or(i == 0, far > 0)))
            def _():
                @pl.loop(0, CHUNKS)
                def _(h):
                    arrived(z0, y0, 1 - c, h)

                first = pl.multiple_of(index(z0, y0, 0) * rows, 2 * rows)
                stage[z0 * lines + y0] = dot(qb[...], held[pl.ds(first, 2 * rows), :], NT)
                out_copy(z0, y0).start()

    own_copy.wait()

    @pl.loop(0, slots)
    def _(k):
        step = lax.div(k, CHUNKS)
        h = lax.rem(k, CHUNKS)
        for side in (1, -1):
            z_line = z + side * (step + 1)

            @pl.when(inside(z_line))
            def _():
                arrived(z_line, y, c, h)
                send_z(z_line, y, h)
                send_y(z_line, y, h)
                send_twin(z_line, y, h)

        if lines == 2:
            for side in (1, -1):
                z_cross = z + side * step
                wanted = jnp.logical_or(step > 1, jnp.logical_or(step == 0, h >= crossed))
                if side == -1:
                    wanted = jnp.logical_and(wanted, step > 0)

                @pl.when(jnp.logical_and(wanted, inside(z_cross)))
                def _():
                    arrived(z_cross, 1 - y, c, h)
                    send_twin(z_cross, 1 - y, h)

            @pl.when(k == slots - CHUNKS)
            def _():
                @pl.loop(0, crossed)
                def _(i):
                    send_z(z, 1 - y, i)

        @pl.when(k < spin // 2)
        def _():
            @pl.loop(0, ITEMS)
            def _(i):
                forward(k * ITEMS + i)

        @pl.when(jnp.logical_and(k >= spin // 2, k < spin))
        def _():
            @pl.loop(0, ITEMS)
            def _(i):
                back((k - spin // 2) * ITEMS + i)

        @pl.when(k == spin)
        def _():
            @pl.loop(1, n)
            def _(j):
                part_to(j).start()

        @pl.when(k == spin + CHUNKS)
        def _():
            @pl.loop(1, n)
            def _(j):
                s = lax.rem(me + j, n)
                pltpu.make_async_remote_copy(
                    src_ref=qsum.at[s],
                    dst_ref=qpart.at[s],
                    send_sem=qpart_send.at[j],
                    recv_sem=qpart_recv.at[s],
                    device_id={"blk": s},
                    device_id_type=MESH,
                ).wait_recv()
                part_to(j).wait_send()

            qpart[me] = qsum[me]
            added = qpart[0]
            for s in range(1, n):
                added = added + qpart[s]
            qtotal[me] = added
            share(qtotal, qsum_send, qsum_recv)

        @pl.when(k == spin + 2 * CHUNKS - 1)
        def _():
            collect(qtotal, qsum_send, qsum_recv)
            total = jnp.concatenate([qtotal[s] for s in range(n)], axis=1)
            high = total.astype(BF16)
            rest = total - high.astype(F32)
            middle = rest.astype(BF16)
            low = (rest - middle.astype(F32)).astype(BF16)
            mine = held[pl.ds(pl.multiple_of(me * rows, rows), rows), :]
            count = 16
            sums = jnp.zeros((1, rows), F32)
            for part in (low, middle, high):
                full = jnp.broadcast_to(part.astype(F32), (count, width)).astype(BF16)
                sums = sums + dot(full, mine, NT)[0:1, :]
            csum[me] = sums * (1.0 / float(queries) ** 0.5)
            share(csum, csum_send, csum_recv)

        early = k - spin
        by_arrival = jnp.logical_and(
            early > 2, jnp.logical_and(h == CHUNKS - 1, step + 1 < depth)
        )
        far = jnp.where(early > 2, step + 1, early)
        use = jnp.logical_or(jnp.logical_and(early >= 0, early <= 2), by_arrival)
        y_score = y
        if lines == 2:
            other = jnp.logical_or(k == spin + CHUNKS, k == spin + CHUNKS + 1)
            far = jnp.where(k == spin + CHUNKS, 0, jnp.where(k == spin + CHUNKS + 1, 2, far))
            y_score = jnp.where(other, 1 - y, y)
            use = jnp.logical_or(use, other)

        @pl.when(use)
        def _():
            score(far, y_score)

    if lines == 2:
        for side in (1, -1):

            @pl.when(jnp.logical_and(z + side >= 0, z + side < depth))
            def _():
                @pl.loop(0, crossed)
                def _(h):
                    arrived(z + side, 1 - y, c, h)
                    send_twin(z + side, 1 - y, h)

        @pl.loop(0, 2)
        def _(j):
            score(3 - 2 * j, 1 - y)

    collect(csum, csum_send, csum_recv)
    ids = (
        lax.broadcasted_iota(jnp.int32, (rows, rows), 0) + me * rows
    ).astype(F32)
    picked = jnp.zeros((rows, rows), F32)
    for s in range(n):
        picked = picked + jnp.where(smalls[s, per - 1 : per, :] == ids, csum[s], 0.0)
    totals_ref[...] = jnp.sum(picked.T, axis=0, keepdims=True)

    @pl.loop(0, depth * lines)
    def _(s):
        z0 = lax.div(s, lines)
        y0 = lax.rem(s, lines)
        out_copy(z0, y0).wait()

        @pl.loop(0, CHUNKS)
        def _(h):
            up, down, over = ways(z0, y0, h)

            @pl.when(up)
            def _():
                moved(0, z0, y0, c, h, up_target).wait_send()

            @pl.when(down)
            def _():
                moved(1, z0, y0, c, h, down_target).wait_send()

            if lines == 2:

                @pl.when(over)
                def _():
                    moved(2, z0, y0, c, h, over_target).wait_send()

            moved(3, z0, y0, c, h, twin).wait_send()


def per_device(n, lines, query_sketch, train_sketch, train_ids, basis_in, basis_out, eig_in, eig_out):
    width = FOUT * FIN
    queries, rows = query_sketch.shape[0], train_sketch.shape[0]
    sources = n // 2
    dma = pltpu.SemaphoreType.DMA
    vmem = pl.BlockSpec(memory_space=pltpu.VMEM)
    hbm = pl.BlockSpec(memory_space=pl.ANY)
    scores, totals = pl.pallas_call(
        functools.partial(kernel, n, lines),
        out_shape=(
            jax.ShapeDtypeStruct((queries, rows * n), F32),
            jax.ShapeDtypeStruct((1, rows), F32),
        ),
        in_specs=[hbm, hbm, vmem, vmem, vmem, vmem, pl.BlockSpec(memory_space=pltpu.SMEM)],
        out_specs=(hbm, vmem),
        scratch_shapes=[
            pltpu.VMEM((n * rows, width), BF16),
            pltpu.VMEM((queries, width), BF16),
            pltpu.VMEM((queries, width), BF16),
            pltpu.VMEM((width, LANES), BF16),
            pltpu.VMEM((2, FOUT, width), F32),
            pltpu.VMEM((1, width), F32),
            pltpu.VMEM((2, LANES, LANES), BF16),
            pltpu.VMEM((sources, queries, 2 * rows), F32),
            pltpu.VMEM((FIN, 128), F32),
            pltpu.VMEM((n, 8, 128), F32),
            pltpu.VMEM((n, 1, width // n), F32),
            pltpu.VMEM((n, 1, width // n), F32),
            pltpu.VMEM((n, 1, width // n), F32),
            pltpu.VMEM((n, 1, rows), F32),
            dma((n * CHUNKS,)),
            dma((4, sources * CHUNKS)),
            dma((n,)),
            dma((n,)),
            dma((n,)),
            dma((n,)),
            dma((n,)),
            dma((n,)),
            dma((n,)),
            dma((n,)),
            dma((2,)),
            dma((sources,)),
        ],
        compiler_params=pltpu.CompilerParams(
            collective_id=0, has_side_effects=True, vmem_limit_bytes=58 * 1024 * 1024
        ),
        cost_estimate=pl.CostEstimate(
            flops=2 * queries * width * (rows * n + 2 * width),
            bytes_accessed=2 * queries * width + 4 * queries * rows * n,
            transcendentals=0,
        ),
    )(
        query_sketch, train_sketch, basis_in, basis_out,
        train_ids.reshape(1, rows), eig_in.reshape(1, FIN), eig_out.reshape(1, FOUT),
    )
    return scores, totals.reshape(rows)


def solution(mesh):
    placed = (
        P(("grp", "blk"), None),
        P(("grp", "blk"), None),
        P(("grp", "blk")),
        P("blk", None),
        P("blk", None),
        P(),
        P(),
    )
    lines = 2 if mesh.shape["grp"] == 2 else 1
    return jax.shard_map(
        functools.partial(per_device, mesh.shape["blk"], lines),
        mesh=mesh,
        in_specs=placed,
        out_specs=(P(("grp", "blk"), None), P(("grp", "blk"))),
        check_vma=False,
    )
```
